128 devices in a mesh: dp: 16 (over z, x_lo, core), head: 8 (over y, x_hi).
Axes of the slice: x: 4 (x_hi: 2, x_lo: 2; x = x_hi * 2 + x_lo), y: 4, z: 4, core: 2. Of those that a mesh axis runs over, the one named last changes fastest.
Arguments:
- latents: bfloat16 [16, 1024, 3072], P('head', 'dp'), may hold values from -6 to 6
- noise: bfloat16 [16, 1024, 3072], P('head', 'dp'), may hold values from -6 to 6
- tsteps: int32 [16], replicated, may hold values from 20 to 979
- text: bfloat16 [16, 512, 3072], P('dp'), may hold values from -6 to 6
- teacher_qkv: bfloat16 [3, 3072, 3072], P(None, None, 'head'), may hold values from -3 to 3
- teacher_out: bfloat16 [3072, 3072], P('head'), may hold values from -1.5 to 1.5
- teacher_mod: bfloat16 [256, 6144], replicated, may hold values from -0.375 to 0.375
- critic_qkv: bfloat16 [3, 3072, 3072], P(None, 'dp', 'head'), may hold values from -3 to 3
- critic_out: bfloat16 [3072, 3072], P('head', 'dp'), may hold values from -1.5 to 1.5
- critic_mod: bfloat16 [256, 6144], replicated, may hold values from -0.375 to 0.375
Outputs:
- score_diff: bfloat16 [16, 1024, 3072], P('dp', 'head')
The draws below stay inside these ranges and needn't reach their ends.
All inputs are finite; a program needn't handle non-finite values.
Results may differ from the reference program's by a relative error of at most 0.017.
Values may be sent and summed in bfloat16 or wider, within the bound.
No kernel may reach another device: no remote copies, remote signals or barrier semaphores. Data moves between devices by JAX's collectives and lax.ppermute only.
A program may use at most 192 MiB of HBM per device.

```python
import math
import jax
import jax.numpy as jnp
from jax import lax

D = 3072
HEAD_DIM = 128
L = 1024
TXT = 512
EMB = 256
B = 16


def drawn_tokens(key):
    fresh = jax.random.truncated_normal(key, -6.0, 6.0, (B, L, D), jnp.float32)
    return fresh.astype(jnp.bfloat16)


def draw_latents(key, part):
    key = jax.random.fold_in(key, 21)
    return drawn_tokens(key)


def draw_noise(key, part):
    key = jax.random.fold_in(key, 22)
    return drawn_tokens(key)


def projection_base(key):
    return jax.random.truncated_normal(key, -3.0, 3.0, (3, D, D), jnp.float32) / D ** 0.5


def draw_teacher_qkv(key, part):
    key = jax.random.fold_in(key, 11)
    base = projection_base(jax.random.fold_in(key, 3))
    return base.astype(jnp.bfloat16)


def draw_critic_qkv(key, part):
    key = jax.random.fold_in(key, 12)
    base = projection_base(jax.random.fold_in(key, 3))
    return base.astype(jnp.bfloat16)


def with_ends(result, own_key, least, top_value):
    index_at = [jax.random.randint(jax.random.fold_in(own_key, axis), (), 0, length) for axis, length in enumerate(result.shape)]
    longest = result.shape.index(max(result.shape))
    next_to = index_at[:longest] + [(index_at[longest] + 1) % result.shape[longest]] + index_at[longest + 1:]
    return result.at[tuple(index_at)].set(least).at[tuple(next_to)].set(top_value)


def level_of(own_key, shape, split, least, top_value):
    loudness = 1.0
    for dim, parts in split:
        steps = jax.random.uniform(jax.random.fold_in(jax.random.fold_in(own_key, 6), dim), (parts,), jnp.float32, least / len(split), top_value / len(split))
        loudness = loudness * jnp.repeat(jnp.exp(steps), shape[dim] // parts).reshape((-1,) + (1,) * (len(shape) - 1 - dim))
    return loudness


def bell_draw(key, dims, deviation, reach, split=(), kind=jnp.bfloat16):
    result = deviation * jax.random.normal(key, dims, jnp.float32)
    if split:
        result = result * level_of(key, dims, split, -0.22, 0.18)
    return jnp.clip(result, -reach, reach).astype(kind)


def setup_inputs(seed: int = 0) -> dict:
    key_list = jax.random.split(jax.random.key(seed), 11)
    latents = draw_latents(jax.random.fold_in(key_list[10], 71), 0)
    noise = draw_noise(jax.random.fold_in(key_list[10], 71), 0)
    tsteps = with_ends(jax.random.randint(key_list[2], (B,), 20, 980), jax.random.fold_in(key_list[2], 1), 20, 979).astype(jnp.int32)
    text = bell_draw(key_list[3], (B, TXT, D), 1.0, 6.0, ((0, 16),))
    teacher_qkv = draw_teacher_qkv(jax.random.fold_in(key_list[10], 71), 0)
    teacher_out = bell_draw(key_list[5], (D, D), (HEAD_DIM // 8) ** -0.5, 1.5, ((0, 8),))
    teacher_mod = bell_draw(key_list[6], (EMB, 2 * D), EMB ** -0.5, 0.375)
    critic_qkv = draw_critic_qkv(jax.random.fold_in(key_list[10], 71), 0)
    critic_out = bell_draw(key_list[8], (D, D), (HEAD_DIM // 8) ** -0.5, 1.5, ((0, 8), (1, 16)))
    critic_mod = bell_draw(key_list[9], (EMB, 2 * D), EMB ** -0.5, 0.375)
    return dict(latents=latents, noise=noise, tsteps=tsteps, text=text, teacher_qkv=teacher_qkv, teacher_out=teacher_out, teacher_mod=teacher_mod, critic_qkv=critic_qkv, critic_out=critic_out, critic_mod=critic_mod)


def embed(tvals, width):
    half = width // 2
    freqs = jnp.exp(-math.log(10000.0) * jnp.arange(half, dtype=jnp.float32) / half)
    angle = tvals.astype(jnp.float32)[:, None] * freqs[None, :]
    return jnp.concatenate([jnp.cos(angle), jnp.sin(angle)], axis=1)

def modulate(joint, temb, w_mod):
    width = joint.shape[1]
    act = jax.nn.silu(temb).astype(jnp.bfloat16)
    mod = jnp.dot(act, w_mod, preferred_element_type=jnp.float32)
    shift = mod[:, :width]
    scale = mod[:, width:]
    rows = joint.astype(jnp.float32)
    mean = lax.optimization_barrier(jnp.mean(rows, axis=1, keepdims=True))
    var = lax.optimization_barrier(jnp.mean(jnp.square(rows - mean), axis=1, keepdims=True))
    norm = (rows - mean) * lax.rsqrt(var + 1e-06)
    return (norm * (1.0 + scale) + shift).astype(jnp.bfloat16)

def attend(query, keys, values, head_dim):
    heads = query.shape[1] // head_dim
    q3 = query.reshape(query.shape[0], heads, head_dim)
    k3 = keys.reshape(keys.shape[0], heads, head_dim)
    v3 = values.reshape(values.shape[0], heads, head_dim)
    scores = jnp.einsum('qhd,khd->hqk', q3, k3, preferred_element_type=jnp.float32) / math.sqrt(head_dim)
    probs = jax.nn.softmax(scores, axis=-1).astype(jnp.bfloat16)
    outs = jnp.einsum('hqk,khd->qhd', probs, v3, preferred_element_type=jnp.float32)
    return outs.astype(jnp.bfloat16).reshape(query.shape[0], heads * head_dim)

def predict(joint, temb, w_qkv, w_out, w_mod):
    hidden = modulate(joint, temb, w_mod)
    query = jnp.dot(hidden[TXT:], w_qkv[0], preferred_element_type=jnp.float32).astype(jnp.bfloat16)
    keys = jnp.dot(hidden, w_qkv[1], preferred_element_type=jnp.float32).astype(jnp.bfloat16)
    values = jnp.dot(hidden, w_qkv[2], preferred_element_type=jnp.float32).astype(jnp.bfloat16)
    mixed = attend(query, keys, values, HEAD_DIM)
    return jnp.dot(mixed, w_out, preferred_element_type=jnp.float32)

def reference(latents, noise, tsteps, text, teacher_qkv, teacher_out, teacher_mod, critic_qkv, critic_out, critic_mod):
    sigma = (tsteps.astype(jnp.float32) / 1000.0)[:, None, None]
    noisy = ((1.0 - sigma) * latents.astype(jnp.float32) + sigma * noise.astype(jnp.float32)).astype(jnp.bfloat16)

    def one_image(items):
        rows, words, tval = items
        joint = jnp.concatenate([words, rows], axis=0)
        temb = embed(tval[None], EMB)
        teacher = predict(joint, temb, teacher_qkv, teacher_out, teacher_mod)
        critic = predict(joint, temb, critic_qkv, critic_out, critic_mod)
        return (critic - teacher).astype(jnp.bfloat16)
    return lax.map(one_image, (noisy, text, tsteps))
```

```python
import functools
import math

import jax
import jax.numpy as jnp
from jax import lax
from jax.experimental import pallas as pl
from jax.experimental.pallas import tpu as pltpu
from jax.sharding import PartitionSpec as P

HEAD_DIM = 128
BLOCK = 128
HALF = 64
F32 = jnp.float32
BF16 = jnp.bfloat16
MIB = 1 << 20


def embed(tvals, width):
    half = width // 2
    freqs = jnp.exp(-math.log(10000.0) * jnp.arange(half, dtype=F32) / half)
    angle = tvals.astype(F32)[:, None] * freqs[None, :]
    return jnp.concatenate([jnp.cos(angle), jnp.sin(angle)], axis=1)


def modulation(temb, w_mod):
    act = jax.nn.silu(temb).astype(BF16)
    mod = jnp.dot(act, w_mod, preferred_element_type=F32)
    return mod.reshape(2, w_mod.shape[1] // 2)


def project_kernel(sizes, chunk, *refs):
    xs, (mod_ref, w_ref, o_ref, h_ref) = refs[: len(sizes)], refs[len(sizes) :]

    @pl.when(pl.program_id(0) == 0)
    def _():
        shift = mod_ref[0:1, :]
        gain = 1.0 + mod_ref[1:2, :]
        base = 0
        for x_ref, size in zip(xs, sizes):

            def step(i, _, x_ref=x_ref, base=base):
                start = pl.multiple_of(i * chunk, chunk)
                rows = x_ref[pl.ds(start, chunk), :].astype(F32)
                mean = jnp.mean(rows, axis=1, keepdims=True)
                rows = rows - mean
                var = jnp.mean(rows * rows, axis=1, keepdims=True)
                norm = rows * lax.rsqrt(var + 1e-06)
                h_ref[pl.ds(pl.multiple_of(base + start, chunk), chunk), :] = (
                    norm * gain + shift
                ).astype(BF16)
                return 0

            lax.fori_loop(0, size // chunk, step, 0)
            base += size

    o_ref[0] = jnp.dot(h_ref[...], w_ref[0], preferred_element_type=F32).astype(BF16)


def project(blocks, mod, weights, first):
    sizes = [b.shape[0] for b in blocks]
    rows, width = sum(sizes), blocks[0].shape[1]
    count, columns = weights.shape[0] - first, weights.shape[2]
    whole = [pl.BlockSpec(b.shape, lambda j: (0, 0)) for b in blocks]
    return pl.pallas_call(
        functools.partial(project_kernel, sizes, 16),
        out_shape=jax.ShapeDtypeStruct((count, rows, columns), BF16),
        grid=(count,),
        in_specs=whole
        + [
            pl.BlockSpec((2, width), lambda j: (0, 0)),
            pl.BlockSpec((1, width, columns), lambda j: (j + first, 0, 0)),
        ],
        out_specs=pl.BlockSpec((1, rows, columns), lambda j: (j, 0, 0)),
        scratch_shapes=[pltpu.VMEM((rows, width), BF16)],
        compiler_params=pltpu.CompilerParams(vmem_limit_bytes=40 * MIB),
        cost_estimate=pl.CostEstimate(
            flops=2 * rows * width * columns * count,
            bytes_accessed=2 * (rows * width + count * width * columns),
            transcendentals=0,
        ),
        name="project",
    )(*blocks, mod, weights)


def attend_kernel(places, groups, *refs):
    critic, teacher = refs[:groups], refs[groups : 2 * groups]
    wc_ref, wt_ref = refs[2 * groups : 2 * groups + 2]
    outs = refs[2 * groups + 2 : -1]
    o_ref = refs[-1]
    columns = wc_ref.shape[0]
    factor = math.log2(math.e) / math.sqrt(HEAD_DIM)
    for m, model in enumerate((critic, teacher)):
        for head in range(columns // HEAD_DIM):
            at = pl.ds(head * HEAD_DIM, HEAD_DIM)
            query = jnp.concatenate(
                [model[g][0, pl.ds(row, BLOCK), at] for g, row in places], axis=0
            )
            scores = [
                lax.dot_general(
                    query,
                    ref[ref.shape[0] - 2, :, at],
                    (((1,), (1,)), ((), ())),
                    preferred_element_type=F32,
                )
                for ref in model
            ]
            top = functools.reduce(
                jnp.maximum, [jnp.max(s, axis=1, keepdims=True) for s in scores]
            )
            total = 0.0
            mixed = 0.0
            for s, ref in zip(scores, model):
                prob = jnp.exp2((s - top) * factor)
                total = total + jnp.sum(prob, axis=1, keepdims=True)
                mixed = mixed + jnp.dot(
                    prob.astype(BF16),
                    ref[ref.shape[0] - 1, :, at],
                    preferred_element_type=F32,
                )
            o_ref[:, pl.ds(m * columns + head * HEAD_DIM, HEAD_DIM)] = (
                mixed / total
            ).astype(BF16)
    width = wc_ref.shape[1]
    part = width // 4
    for j in range(4):
        at = pl.ds(j * part, part)
        diff = jnp.dot(
            o_ref[:, :columns], wc_ref[:, at], preferred_element_type=F32
        ) - jnp.dot(o_ref[:, columns:], wt_ref[:, at], preferred_element_type=F32)
        for i, out in enumerate(outs):
            out[:, at] = diff[i * HALF : (i + 1) * HALF].astype(out.dtype)


def attend(places, critic, teacher, wc, wt):
    rows = BLOCK * len(places)
    columns, width = wc.shape
    keys = sum(g.shape[1] for g in critic)
    return pl.pallas_call(
        functools.partial(attend_kernel, places, len(critic)),
        out_shape=[jax.ShapeDtypeStruct((HALF, width), BF16)] * (rows // HALF),
        scratch_shapes=[pltpu.VMEM((rows, 2 * columns), BF16)],
        compiler_params=pltpu.CompilerParams(vmem_limit_bytes=48 * MIB),
        cost_estimate=pl.CostEstimate(
            flops=8 * rows * columns * (2 * keys + width),
            bytes_accessed=2 * (6 * keys * columns + 2 * columns * width + rows * width),
            transcendentals=6 * rows * keys,
        ),
        name="attend",
    )(*critic, *teacher, wc, wt)


def shards(
    latents,
    noise,
    tsteps,
    text,
    teacher_qkv,
    teacher_out,
    teacher_mod,
    critic_qkv,
    critic_out,
    critic_mod,
):
    images = latents.shape[0]
    n_dp, n_head = lax.axis_size("dp"), lax.axis_size("head")
    dp, head = lax.axis_index("dp"), lax.axis_index("head")
    core = dp % 2

    wc_qkv = lax.all_gather(critic_qkv, "dp", axis=1, tiled=True)
    wc_out = lax.all_gather(critic_out, "dp", axis=1, tiled=True)

    local_times = lax.dynamic_slice_in_dim(tsteps, head * images, images)
    sigma = (local_times.astype(F32) / 1000.0)[:, None, None]
    noisy = ((1.0 - sigma) * latents.astype(F32) + sigma * noise.astype(F32)).astype(BF16)

    def cross(flip):
        return [
            (d * n_head + h, (2 * h + (d % 2) ^ flip) * n_head + d // 2)
            for d in range(n_dp)
            for h in range(n_head)
        ]

    first = jnp.where(core == 0, noisy[0], noisy[1])
    second = jnp.where(core == 0, noisy[1], noisy[0])
    own = jnp.concatenate(
        [
            lax.ppermute(first, ("dp", "head"), cross(0)),
            lax.ppermute(second, ("dp", "head"), cross(1)),
        ],
        axis=0,
    )

    up = [(i, (i + 2) % n_head) for i in range(n_head)]
    down = [(i, (i - 2) % n_head) for i in range(n_head)]
    swap = [(i, i ^ 1) for i in range(n_head)]

    def go(x, perm):
        return lax.ppermute(x, "head", perm)

    own_below, own_above = go(own, up), go(own, down)
    other = go(own, swap)
    far_a, far_b = go(own_below[:HALF], up), go(own_above[HALF:], down)
    other_below, other_above = go(other, up), go(other, down)
    other_far_a = go(other_below[:HALF], up)
    other_far_b = go(other_above[HALF:], down)

    own_time = lax.dynamic_slice_in_dim(tsteps, dp, 1)
    temb = embed(own_time, teacher_mod.shape[0])
    arrivals = [
        [own, own_below, own_above, other],
        [far_a, far_b, other_below, other_above],
        [other_far_a, other_far_b],
    ]

    def keyed(w, w_mod):
        mod = modulation(temb, w_mod)
        return [project([text[0]], mod, w, 1)] + [project(a, mod, w, 0) for a in arrivals]

    teacher = keyed(teacher_qkv, teacher_mod)
    critic = keyed(wc_qkv, critic_mod)

    far = [(3, 0), (2, 0)]
    near_other = [(2, BLOCK), (2, 2 * BLOCK)]
    near_own = [(1, BLOCK), (1, 2 * BLOCK)]
    here = [(1, 3 * BLOCK), (1, 0)]

    def run(places):
        return attend(places, critic, teacher, wc_out, teacher_out)

    def add(*parts):
        return functools.reduce(jnp.add, [p.astype(F32) for p in parts]).astype(BF16)

    fo_a, fo_b, f_a, f_b = run(far)
    via_o_a, via_o_b = go(fo_a, up), go(fo_b, down)
    via_a, via_b = go(f_a, up), go(f_b, down)
    ob_a, ob_b, oa_a, oa_b = run(near_other)
    so_below_a, so_above_b = go(ob_a, down), go(oa_b, up)
    so_below_b, so_above_a = go(add(ob_b, via_o_b), down), go(add(oa_a, via_o_a), up)
    nb_a, nb_b, na_a, na_b = run(near_own)
    s_below_a, s_above_b = go(nb_a, down), go(na_b, up)
    s_below_b, s_above_a = go(add(nb_b, via_b), down), go(add(na_a, via_a), up)
    ho_a, ho_b, h_a, h_b = run(here)
    cross_a = go(add(ho_a, so_below_a, so_above_a), swap)
    cross_b = go(add(ho_b, so_below_b, so_above_b), swap)
    top = add(h_a, s_below_a, s_above_a, cross_a)
    low = add(h_b, s_below_b, s_above_b, cross_b)
    out = jnp.where(
        core == 0,
        jnp.concatenate([top, low], axis=0),
        jnp.concatenate([low, top], axis=0),
    )
    return out[None]


def solution(mesh):
    in_specs = (
        P("head", "dp", None),
        P("head", "dp", None),
        P(),
        P("dp", None, None),
        P(None, None, "head"),
        P("head", None),
        P(),
        P(None, "dp", "head"),
        P("head", "dp"),
        P(),
    )
    out_specs = P("dp", "head", None)
    return jax.shard_map(shards, mesh=mesh, in_specs=in_specs, out_specs=out_specs, check_vma=False)
```

```python
import functools
import math

import jax
import jax.numpy as jnp
from jax import lax
from jax.experimental import pallas as pl
from jax.experimental.pallas import tpu as pltpu
from jax.sharding import PartitionSpec as P

HEAD_DIM = 128
HALF = 64
F32 = jnp.float32
BF16 = jnp.bfloat16
VMEM = 16 << 20
CHUNK = 64


def embed(tvals, width):
    half = width // 2
    freqs = jnp.exp(-math.log(10000.0) * jnp.arange(half, dtype=F32) / half)
    angle = tvals.astype(F32)[:, None] * freqs[None, :]
    return jnp.concatenate([jnp.cos(angle), jnp.sin(angle)], axis=1)


def modulation(temb, w_mod):
    act = jax.nn.silu(temb).astype(BF16)
    mod = jnp.dot(act, w_mod, preferred_element_type=F32)
    return mod.reshape(2, w_mod.shape[1] // 2)


def normalise(x_ref, mods, outs, base, size, chunk):
    def step(i, _):
        start = pl.multiple_of(i * chunk, chunk)
        rows = x_ref[pl.ds(start, chunk), :].astype(F32)
        pivot = rows[:, 0:1]
        away = rows - pivot
        mean = jnp.mean(away, axis=1, keepdims=True)
        var = jnp.maximum(jnp.mean(away * away, axis=1, keepdims=True) - mean * mean, 0.0)
        scale = lax.rsqrt(var + 1e-06)
        norm = (x_ref[pl.ds(start, chunk), :].astype(F32) - (pivot + mean)) * scale
        at = pl.ds(pl.multiple_of(base + start, chunk), chunk)
        for mod_ref, h_ref in zip(mods, outs):
            h_ref[at, :] = (norm * (1.0 + mod_ref[1:2, :]) + mod_ref[0:1, :]).astype(BF16)
        return 0

    lax.fori_loop(0, size // chunk, step, 0)


def write_projections(h, weights, o_ref):
    columns = o_ref.shape[1] // len(weights)
    for j, w in enumerate(weights):
        out = jnp.dot(h, w, preferred_element_type=F32)
        if j == 0 and len(weights) == 3:
            out = out * (math.log2(math.e) / math.sqrt(HEAD_DIM))
        o_ref[:, j * columns : (j + 1) * columns] = out.astype(BF16)


def teacher_kernel(sizes, first, *refs):
    xs, refs = refs[: len(sizes)], refs[len(sizes) :]
    mods, (w_ref, o_ref, hc_ref, h_ref) = refs[:2], refs[2:]
    base = 0
    for x_ref, size in zip(xs, sizes):
        normalise(x_ref, mods, (h_ref, hc_ref), base, size, CHUNK)
        base += size
    write_projections(h_ref[...], [w_ref[j] for j in range(first, 3)], o_ref)


def teacher_project(blocks, mods, weights, first):
    sizes = [b.shape[0] for b in blocks]
    rows, width = sum(sizes), blocks[0].shape[1]
    count, columns = 3 - first, weights.shape[2]
    return pl.pallas_call(
        functools.partial(teacher_kernel, sizes, first),
        out_shape=[
            jax.ShapeDtypeStruct((rows, count * columns), BF16),
            jax.ShapeDtypeStruct((rows, width), BF16),
        ],
        scratch_shapes=[pltpu.VMEM((rows, width), BF16)],
        compiler_params=pltpu.CompilerParams(vmem_limit_bytes=VMEM),
        cost_estimate=pl.CostEstimate(
            flops=4 * rows * width * columns * count,
            bytes_accessed=4 * rows * width + 6 * width * columns,
            transcendentals=0,
        ),
        name="teacher_project",
    )(*blocks, *mods, weights)


def critic_kernel(first, h_ref, w_ref, o_ref):
    width = h_ref.shape[1]
    write_projections(
        h_ref[...], [w_ref[:, j].reshape(width, -1) for j in range(first, 3)], o_ref
    )


def critic_project(h, weights, first):
    rows, width = h.shape
    count, columns = 3 - first, weights.shape[3]
    return pl.pallas_call(
        functools.partial(critic_kernel, first),
        out_shape=jax.ShapeDtypeStruct((rows, count * columns), BF16),
        compiler_params=pltpu.CompilerParams(vmem_limit_bytes=VMEM),
        cost_estimate=pl.CostEstimate(
            flops=4 * rows * width * columns * count,
            bytes_accessed=2 * rows * width + 2 * weights.size,
            transcendentals=0,
        ),
        name="critic_project",
    )(h, weights)


def attend_kernel(places, groups, sums, *refs):
    models, (wt_ref, wc_ref), refs = (
        (refs[:groups], refs[groups : 2 * groups]),
        refs[2 * groups : 2 * groups + 2],
        refs[2 * groups + 2 :],
    )
    arrived, outs, o_ref = refs[: len(sums)], refs[len(sums) : -1], refs[-1]
    columns, width = wt_ref.shape
    for m, keyed in enumerate(models):
        for head in range(columns // HEAD_DIM):
            base = head * HEAD_DIM
            query = jnp.concatenate(
                [keyed[g][pl.ds(row, HALF), pl.ds(base, HEAD_DIM)] for g, row in places], axis=0
            )
            parts = [
                [
                    ref[:, pl.ds(ref.shape[1] - n * columns + base, HEAD_DIM)]
                    for n in (2, 1)
                ]
                for ref in keyed
            ]
            scores = [
                lax.dot_general(
                    query, k, (((1,), (1,)), ((), ())), preferred_element_type=F32
                )
                for k, _ in parts
            ]
            top = functools.reduce(
                jnp.maximum, [jnp.max(s, axis=1, keepdims=True) for s in scores]
            )
            mixed = 0.0
            for s, (_, v) in zip(scores, parts):
                prob = jnp.exp2(s - top).astype(BF16)
                with_ones = jnp.concatenate([v, jnp.ones_like(v)], axis=1)
                mixed = mixed + jnp.dot(prob, with_ones, preferred_element_type=F32)
            o_ref[:, pl.ds(m * columns + head * HEAD_DIM, HEAD_DIM)] = (
                mixed[:, :HEAD_DIM] / mixed[:, HEAD_DIM:]
            ).astype(BF16)
    critic = wc_ref[...].reshape(width, columns)
    part = width // 4
    for j in range(4):
        at = pl.ds(j * part, part)
        diff = lax.dot_general(
            o_ref[:, columns:],
            critic[j * part : (j + 1) * part],
            (((1,), (1,)), ((), ())),
            preferred_element_type=F32,
        ) - jnp.dot(o_ref[:, :columns], wt_ref[:, at], preferred_element_type=F32)
        for i, out in enumerate(outs):
            piece = diff[i * HALF : (i + 1) * HALF]
            if i in sums:
                piece = piece + arrived[sums.index(i)][:, at].astype(F32)
            out[:, at] = piece.astype(out.dtype)


def attend(places, teacher, critic, teacher_out, critic_out, arrived=None):
    arrived = arrived or {}
    rows = HALF * len(places)
    columns, width = teacher_out.shape
    keys = sum(g.shape[0] for g in teacher)

    args = (*teacher, *critic, teacher_out, critic_out, *arrived.values())
    piece = jax.ShapeDtypeStruct((HALF, width), BF16)
    return pl.pallas_call(
        functools.partial(attend_kernel, places, len(teacher), tuple(arrived)),
        out_shape=[piece] * len(places),
        scratch_shapes=[pltpu.VMEM((rows, 2 * columns), BF16)],
        compiler_params=pltpu.CompilerParams(vmem_limit_bytes=VMEM),
        cost_estimate=pl.CostEstimate(
            flops=16 * rows * columns * (2 * keys + width),
            bytes_accessed=2 * (6 * keys * columns + 2 * columns * width + rows * width),
            transcendentals=6 * rows * keys,
        ),
        name="attend",
    )(*args)


def shards(
    latents,
    noise,
    tsteps,
    text,
    teacher_qkv,
    teacher_out,
    teacher_mod,
    critic_qkv,
    critic_out,
    critic_mod,
):
    images = latents.shape[0]
    n_dp, n_head = lax.axis_size("dp"), lax.axis_size("head")
    dp, head = lax.axis_index("dp"), lax.axis_index("head")
    core = dp % 2

    local_times = lax.dynamic_slice_in_dim(tsteps, head * images, images)
    sigma = (local_times.astype(F32) / 1000.0)[:, None, None]
    noisy = ((1.0 - sigma) * latents.astype(F32) + sigma * noise.astype(F32)).astype(BF16)

    def cross(flip):
        return [
            (d * n_head + h, (2 * h + (d % 2) ^ flip) * n_head + d // 2)
            for d in range(n_dp)
            for h in range(n_head)
        ]

    first = jnp.where(core == 0, noisy[0], noisy[1])
    second = jnp.where(core == 0, noisy[1], noisy[0])
    up = [(i, (i + 2) % n_head) for i in range(n_head)]
    down = [(i, (i - 2) % n_head) for i in range(n_head)]
    twice = [(i, (i + 4) % n_head) for i in range(n_head)]
    swap = [(i, i ^ 1) for i in range(n_head)]

    def go(x, perm):
        return lax.ppermute(x, "head", perm)

    fence = lax.optimization_barrier
    own_time = lax.dynamic_slice_in_dim(tsteps, dp, 1)
    temb = embed(own_time, teacher_mod.shape[0])
    mods = [modulation(temb, w) for w in (teacher_mod, critic_mod)]
    w_critic = lax.all_gather(critic_qkv, "dp")


    own_0 = lax.ppermute(first, ("dp", "head"), cross(0))
    text_t, text_h = teacher_project([text[0]], mods, teacher_qkv, 1)
    own_0, text_t, text_h, second = fence((own_0, text_t, text_h, second))

    own_1 = lax.ppermute(second, ("dp", "head"), cross(1))
    below_0, above_0, other_0 = go(own_0, up), go(own_0, down), go(own_0, swap)
    own_0, own_1, below_0, above_0, other_0 = fence((own_0, own_1, below_0, above_0, other_0))

    below_1, above_1, other_1 = go(own_1, up), go(own_1, down), go(own_1, swap)
    far_0, far_1 = go(below_0, up), go(own_1, twice)
    t_1, h_1 = teacher_project([own_0, own_1, below_0, above_0, other_0], mods, teacher_qkv, 0)
    other = jnp.concatenate([other_0, other_1], axis=0)
    far = jnp.concatenate([far_0, far_1], axis=0)
    below_1, above_1, other, far, t_1, text_h = fence((below_1, above_1, other, far, t_1, text_h))

    o_below, o_above, o_far = go(other, up), go(other, down), go(far, swap)
    text_c = critic_project(text_h, w_critic, 1)
    h_1, text_c = fence((h_1, text_c))
    c_1 = critic_project(h_1, w_critic, 0)
    w_critic_out = lax.all_gather(fence((critic_out.T, text_c))[0], "dp")
    below_1, c_1 = fence((below_1, c_1))
    t_2, h_2 = teacher_project([below_1, above_1, other[HALF:], far], mods, teacher_qkv, 0)
    c_2 = critic_project(h_2, w_critic, 0)
    o_below, o_above, o_far, c_2 = fence((o_below, o_above, o_far, c_2))
    t_3, h_3 = teacher_project([o_below, o_above, o_far], mods, teacher_qkv, 0)
    c_3 = critic_project(h_3, w_critic, 0)
    teacher, critic = [text_t, t_1, t_2, t_3], [text_c, c_1, c_2, c_3]

    def run(places, arrived=None):
        places = [(g, HALF * i) for g, i in places]
        return attend(places, teacher, critic, teacher_out, w_critic_out, arrived)

    def add(*parts):
        return functools.reduce(jnp.add, [p.astype(F32) for p in parts]).astype(BF16)

    fo_a, fo_b = run([(3, 4), (3, 5)])
    via_o_a, via_o_b = go(fo_a, up), go(fo_b, down)
    f_a, f_b = run([(2, 3), (2, 4)])
    via_a, via_b = go(f_a, up), go(f_b, down)
    ob_a, ob_b, oa_a, oa_b = run(
        [(3, 0), (3, 1), (3, 2), (3, 3)], {1: via_o_b, 2: via_o_a}
    )
    so_below_b, so_above_a = go(ob_b, down), go(oa_a, up)
    so_below_a, so_above_b = go(ob_a, down), go(oa_b, up)
    nb_a, nb_b, na_a, na_b = run([(1, 2), (2, 0), (1, 3), (2, 1)], {1: via_b, 2: via_a})
    s_below_b, s_above_a = go(nb_b, down), go(na_a, up)
    s_below_a, s_above_b = go(nb_a, down), go(na_b, up)
    *teacher, _ = lax.optimization_barrier((*teacher, nb_a))
    ho_a, ho_b, h_a, h_b = run([(1, 4), (2, 2), (1, 0), (1, 1)])
    cross_a = go(add(ho_a, so_below_a, so_above_a), swap)
    cross_b = go(add(ho_b, so_below_b, so_above_b), swap)
    top = add(h_a, s_below_a, s_above_a, cross_a)
    low = add(h_b, s_below_b, s_above_b, cross_b)
    out = jnp.where(
        core == 0,
        jnp.concatenate([top, low], axis=0),
        jnp.concatenate([low, top], axis=0),
    )
    return out[None]


def solution(mesh):
    in_specs = (
        P("head", "dp", None),
        P("head", "dp", None),
        P(),
        P("dp", None, None),
        P(None, None, "head"),
        P("head", None),
        P(),
        P(None, "dp", "head"),
        P("head", "dp"),
        P(),
    )
    out_specs = P("dp", "head", None)
    return jax.shard_map(shards, mesh=mesh, in_specs=in_specs, out_specs=out_specs, check_vma=False)
```

```python
import functools
import math

import jax
import jax.numpy as jnp
from jax import lax
from jax.experimental import pallas as pl
from jax.experimental.pallas import tpu as pltpu
from jax.sharding import PartitionSpec as P

HEAD_DIM = 128
HALF = 64
F32 = jnp.float32
BF16 = jnp.bfloat16
VMEM = 10 << 20
CHUNK = 64


def embed(tvals, width):
    half = width // 2
    freqs = jnp.exp(-math.log(10000.0) * jnp.arange(half, dtype=F32) / half)
    angle = tvals.astype(F32)[:, None] * freqs[None, :]
    return jnp.concatenate([jnp.cos(angle), jnp.sin(angle)], axis=1)


def modulation(temb, w_mod):
    act = jax.nn.silu(temb).astype(BF16)
    mod = jnp.dot(act, w_mod, preferred_element_type=F32)
    return mod.reshape(2, w_mod.shape[1] // 2)


def normalise(x_ref, mods, outs, base, size, chunk):
    def step(i, _):
        start = pl.multiple_of(i * chunk, chunk)
        rows = x_ref[pl.ds(start, chunk), :].astype(F32)
        pivot = rows[:, 0:1]
        away = rows - pivot
        mean = jnp.mean(away, axis=1, keepdims=True)
        var = jnp.maximum(jnp.mean(away * away, axis=1, keepdims=True) - mean * mean, 0.0)
        scale = lax.rsqrt(var + 1e-06)
        norm = (x_ref[pl.ds(start, chunk), :].astype(F32) - (pivot + mean)) * scale
        at = pl.ds(pl.multiple_of(base + start, chunk), chunk)
        for mod_ref, h_ref in zip(mods, outs):
            h_ref[at, :] = (norm * (1.0 + mod_ref[1:2, :]) + mod_ref[0:1, :]).astype(BF16)
        return 0

    lax.fori_loop(0, size // chunk, step, 0)


def write_projections(h, weights, o_ref):
    columns = o_ref.shape[1] // len(weights)
    for j, w in enumerate(weights):
        out = jnp.dot(h, w, preferred_element_type=F32)
        if j == 0 and len(weights) == 3:
            out = out * (math.log2(math.e) / math.sqrt(HEAD_DIM))
        o_ref[:, j * columns : (j + 1) * columns] = out.astype(BF16)


def teacher_kernel(sizes, first, *refs):
    xs, refs = refs[: len(sizes)], refs[len(sizes) :]
    mods, (w_ref, o_ref, hc_ref, h_ref) = refs[:2], refs[2:]
    base = 0
    for x_ref, size in zip(xs, sizes):
        normalise(x_ref, mods, (h_ref, hc_ref), base, size, CHUNK)
        base += size
    write_projections(h_ref[...], [w_ref[j] for j in range(first, 3)], o_ref)


def teacher_project(blocks, mods, weights, first):
    sizes = [b.shape[0] for b in blocks]
    rows, width = sum(sizes), blocks[0].shape[1]
    count, columns = 3 - first, weights.shape[2]
    return pl.pallas_call(
        functools.partial(teacher_kernel, sizes, first),
        out_shape=[
            jax.ShapeDtypeStruct((rows, count * columns), BF16),
            jax.ShapeDtypeStruct((rows, width), BF16),
        ],
        scratch_shapes=[pltpu.VMEM((rows, width), BF16)],
        compiler_params=pltpu.CompilerParams(vmem_limit_bytes=VMEM),
        cost_estimate=pl.CostEstimate(
            flops=rows * width * columns * count // 4,
            bytes_accessed=rows * width,
            transcendentals=0,
        ),
        name="teacher_project",
    )(*blocks, *mods, weights)


def critic_kernel(first, h_ref, w_ref, o_ref):
    width = h_ref.shape[1]
    write_projections(
        h_ref[...], [w_ref[:, j].reshape(width, -1) for j in range(first, 3)], o_ref
    )


def critic_project(h, weights, first):
    rows, width = h.shape
    count, columns = 3 - first, weights.shape[3]
    return pl.pallas_call(
        functools.partial(critic_kernel, first),
        out_shape=jax.ShapeDtypeStruct((rows, count * columns), BF16),
        compiler_params=pltpu.CompilerParams(vmem_limit_bytes=VMEM),
        cost_estimate=pl.CostEstimate(
            flops=rows * width * columns * count // 4,
            bytes_accessed=rows * width,
            transcendentals=0,
        ),
        name="critic_project",
    )(h, weights)


def attend_kernel(places, groups, sums, *refs):
    models, (wt_ref, wc_ref), refs = (
        (refs[:groups], refs[groups : 2 * groups]),
        refs[2 * groups : 2 * groups + 2],
        refs[2 * groups + 2 :],
    )
    arrived, outs, o_ref = refs[: len(sums)], refs[len(sums) : -1], refs[-1]
    columns, width = wt_ref.shape
    for m, keyed in enumerate(models):
        for head in range(columns // HEAD_DIM):
            base = head * HEAD_DIM
            query = jnp.concatenate(
                [keyed[g][pl.ds(row, HALF), pl.ds(base, HEAD_DIM)] for g, row in places], axis=0
            )
            parts = [
                [
                    ref[:, pl.ds(ref.shape[1] - n * columns + base, HEAD_DIM)]
                    for n in (2, 1)
                ]
                for ref in keyed
            ]
            scores = [
                lax.dot_general(
                    query, k, (((1,), (1,)), ((), ())), preferred_element_type=F32
                )
                for k, _ in parts
            ]
            top = functools.reduce(
                jnp.maximum, [jnp.max(s, axis=1, keepdims=True) for s in scores]
            )
            mixed = 0.0
            for s, (_, v) in zip(scores, parts):
                prob = jnp.exp2(s - top).astype(BF16)
                with_ones = jnp.concatenate([v, jnp.ones_like(v)], axis=1)
                mixed = mixed + jnp.dot(prob, with_ones, preferred_element_type=F32)
            o_ref[:, pl.ds(m * columns + head * HEAD_DIM, HEAD_DIM)] = (
                mixed[:, :HEAD_DIM] / mixed[:, HEAD_DIM:]
            ).astype(BF16)
    critic = wc_ref[...].reshape(width, columns)
    part = width // 4
    for j in range(4):
        at = pl.ds(j * part, part)
        diff = lax.dot_general(
            o_ref[:, columns:],
            critic[j * part : (j + 1) * part],
            (((1,), (1,)), ((), ())),
            preferred_element_type=F32,
        ) - jnp.dot(o_ref[:, :columns], wt_ref[:, at], preferred_element_type=F32)
        for i, arrival in zip(sums, arrived):
            add = arrival[:, at].astype(F32)
            rows = [diff[: i * HALF], diff[i * HALF : (i + 1) * HALF] + add, diff[(i + 1) * HALF :]]
            diff = jnp.concatenate([r for r in rows if r.shape[0]], axis=0)
        base = 0
        for out in outs:
            out[:, at] = diff[base : base + out.shape[0]].astype(out.dtype)
            base += out.shape[0]


def attend(places, split, teacher, critic, teacher_out, critic_out, arrived=None):
    arrived = arrived or {}
    rows = HALF * len(places)
    columns, width = teacher_out.shape
    keys = sum(g.shape[0] for g in teacher)

    args = (*teacher, *critic, teacher_out, critic_out, *arrived.values())
    return pl.pallas_call(
        functools.partial(attend_kernel, places, len(teacher), tuple(arrived)),
        out_shape=[jax.ShapeDtypeStruct((n * HALF, width), BF16) for n in split],
        scratch_shapes=[pltpu.VMEM((rows, 2 * columns), BF16)],
        compiler_params=pltpu.CompilerParams(vmem_limit_bytes=VMEM),
        cost_estimate=pl.CostEstimate(
            flops=8 * rows * columns * (2 * keys + width),
            bytes_accessed=rows * width,
            transcendentals=0,
        ),
        name="attend",
    )(*args)


def shards(
    latents,
    noise,
    tsteps,
    text,
    teacher_qkv,
    teacher_out,
    teacher_mod,
    critic_qkv,
    critic_out,
    critic_mod,
):
    images = latents.shape[0]
    n_dp, n_head = lax.axis_size("dp"), lax.axis_size("head")
    dp, head = lax.axis_index("dp"), lax.axis_index("head")
    core = dp % 2

    local_times = lax.dynamic_slice_in_dim(tsteps, head * images, images)
    sigma = (local_times.astype(F32) / 1000.0)[:, None, None]
    noisy = ((1.0 - sigma) * latents.astype(F32) + sigma * noise.astype(F32)).astype(BF16)

    def cross(flip):
        return [
            (d * n_head + h, (2 * h + (d % 2) ^ flip) * n_head + d // 2)
            for d in range(n_dp)
            for h in range(n_head)
        ]

    first = jnp.where(core == 0, noisy[0], noisy[1])
    second = jnp.where(core == 0, noisy[1], noisy[0])
    up = [(i, (i + 2) % n_head) for i in range(n_head)]
    down = [(i, (i - 2) % n_head) for i in range(n_head)]
    twice = [(i, (i + 4) % n_head) for i in range(n_head)]
    swap = [(i, i ^ 1) for i in range(n_head)]

    def go(x, perm):
        return lax.ppermute(x, "head", perm)

    fence = lax.optimization_barrier
    own_time = lax.dynamic_slice_in_dim(tsteps, dp, 1)
    temb = embed(own_time, teacher_mod.shape[0])
    mods = [modulation(temb, w) for w in (teacher_mod, critic_mod)]
    w_critic = lax.all_gather(critic_qkv, "dp")


    own_0 = lax.ppermute(first, ("dp", "head"), cross(0))
    text_t, text_h = teacher_project([text[0]], mods, teacher_qkv, 1)
    own_0, text_t, text_h = fence((own_0, text_t, text_h))

    own_1 = lax.ppermute(second, ("dp", "head"), cross(1))
    below_0, above_0, other_0 = go(own_0, up), go(own_0, down), go(own_0, swap)
    own_0, own_1, below_0, above_0, other_0 = fence((own_0, own_1, below_0, above_0, other_0))

    below_1, above_1, other_1 = go(own_1, up), go(own_1, down), go(own_1, swap)
    far_0, far_1 = go(below_0, up), go(own_1, twice)
    t_1, h_1 = teacher_project([own_0, own_1, below_0, above_0, other_0], mods, teacher_qkv, 0)
    other = jnp.concatenate([other_0, other_1], axis=0)
    far = jnp.concatenate([far_0, far_1], axis=0)
    below_1, above_1, other, far, t_1, text_h = fence((below_1, above_1, other, far, t_1, text_h))
    w_critic, out_t, text_h = fence((w_critic, critic_out.T, text_h))

    w_critic_out = lax.all_gather(out_t, "dp")
    o_below, o_above, o_far = go(other, up), go(other, down), go(far, swap)
    text_c = critic_project(text_h, w_critic, 1)
    h_1, text_c = fence((h_1, text_c))
    c_1 = critic_project(h_1, w_critic, 0)
    below_1, c_1 = fence((below_1, c_1))
    t_2, h_2 = teacher_project([below_1, above_1, other[HALF:], far], mods, teacher_qkv, 0)
    c_2 = critic_project(h_2, w_critic, 0)
    o_below, o_above, o_far, c_2 = fence((o_below, o_above, o_far, c_2))
    t_3, h_3 = teacher_project([o_below, o_above, o_far], mods, teacher_qkv, 0)
    c_3 = critic_project(h_3, w_critic, 0)
    teacher, critic = [text_t, t_1, t_2, t_3], [text_c, c_1, c_2, c_3]

    def run(places, split, arrived=None):
        places = [(g, HALF * i) for g, i in places]
        return attend(places, split, teacher, critic, teacher_out, w_critic_out, arrived)

    def add(*parts):
        return functools.reduce(jnp.add, [p.astype(F32) for p in parts]).astype(BF16)

    fo_a, fo_b = run([(3, 4), (3, 5)], [1, 1])
    via_o_a, via_o_b = go(fo_a, up), go(fo_b, down)
    *teacher, fo_a = fence((*teacher, fo_a))
    f_a, f_b = run([(2, 3), (2, 4)], [1, 1])
    via_a, via_b = go(f_a, up), go(f_b, down)
    *teacher, f_a = fence((*teacher, f_a))
    ob, oa = run([(3, 0), (3, 1), (3, 2), (3, 3)], [2, 2], {1: via_o_b, 2: via_o_a})
    so_below, so_above = go(ob, down), go(oa, up)
    *teacher, ob = fence((*teacher, ob))
    nb, na = run([(1, 2), (2, 0), (1, 3), (2, 1)], [2, 2], {1: via_b, 2: via_a})
    s_below, s_above = go(nb, down), go(na, up)
    *teacher, _ = fence((*teacher, nb))
    ho, here = run([(1, 4), (2, 2), (1, 0), (1, 1)], [2, 2])
    crossed = go(add(ho, so_below, so_above), swap)
    out = add(here, s_below, s_above, crossed)
    out = jnp.where(core == 0, out, jnp.concatenate([out[HALF:], out[:HALF]], axis=0))
    return out[None]


def solution(mesh):
    in_specs = (
        P("head", "dp", None),
        P("head", "dp", None),
        P(),
        P("dp", None, None),
        P(None, None, "head"),
        P("head", None),
        P(),
        P(None, "dp", "head"),
        P("head", "dp"),
        P(),
    )
    out_specs = P("dp", "head", None)
    return jax.shard_map(shards, mesh=mesh, in_specs=in_specs, out_specs=out_specs, check_vma=False)
```

```python
import functools
import math

import jax
import jax.numpy as jnp
from jax import lax
from jax.experimental import pallas as pl
from jax.experimental.pallas import tpu as pltpu
from jax.sharding import PartitionSpec as P

HEAD_DIM = 128
HALF = 64
F32 = jnp.float32
BF16 = jnp.bfloat16
VMEM = 10 << 20
CHUNK = 64


def embed(tvals, width):
    half = width // 2
    freqs = jnp.exp(-math.log(10000.0) * jnp.arange(half, dtype=F32) / half)
    angle = tvals.astype(F32)[:, None] * freqs[None, :]
    return jnp.concatenate([jnp.cos(angle), jnp.sin(angle)], axis=1)


def modulation(temb, w_mod):
    act = jax.nn.silu(temb).astype(BF16)
    mod = jnp.dot(act, w_mod, preferred_element_type=F32)
    return mod.reshape(2, w_mod.shape[1] // 2)


def normalise(x_ref, mods, outs, base, size, chunk):
    def step(i, _):
        start = pl.multiple_of(i * chunk, chunk)
        rows = x_ref[pl.ds(start, chunk), :].astype(F32)
        pivot = rows[:, 0:1]
        away = rows - pivot
        mean = jnp.mean(away, axis=1, keepdims=True)
        var = jnp.maximum(jnp.mean(away * away, axis=1, keepdims=True) - mean * mean, 0.0)
        scale = lax.rsqrt(var + 1e-06)
        norm = (x_ref[pl.ds(start, chunk), :].astype(F32) - (pivot + mean)) * scale
        at = pl.ds(pl.multiple_of(base + start, chunk), chunk)
        for mod_ref, h_ref in zip(mods, outs):
            h_ref[at, :] = (norm * (1.0 + mod_ref[1:2, :]) + mod_ref[0:1, :]).astype(BF16)
        return 0

    lax.fori_loop(0, size // chunk, step, 0)


def write_projections(h_ref, weight_of, first, o_ref, row):
    columns = weight_of(0).shape[1]
    before = o_ref.shape[1] - 3 * columns

    def step(j, _):
        out = jnp.dot(h_ref[...], weight_of(j), preferred_element_type=F32)
        if first == 0:
            out = out * jnp.where(j == 0, math.log2(math.e) / math.sqrt(HEAD_DIM), 1.0)
        at = pl.ds(pl.multiple_of(j * columns + before, columns), columns)
        o_ref[row : row + h_ref.shape[0], at] = out.astype(BF16)
        return 0

    lax.fori_loop(first, 3, step, 0)


def teacher_kernel(sizes, kept, *refs):
    xs, refs = refs[: len(sizes)], refs[len(sizes) :]
    mods, w_ref, refs = refs[:2], refs[2], refs[3:]
    olds, (o_ref, hc_ref, h_ref) = refs[:kept], refs[kept:]
    base = 0
    for x_ref, size in zip(xs, sizes):
        normalise(x_ref, mods, (h_ref, hc_ref), base, size, CHUNK)
        base += size
    row = 0
    for old in olds:
        o_ref[row : row + old.shape[0], o_ref.shape[1] - old.shape[1] :] = old[...]
        row += old.shape[0]
    first = 3 - o_ref.shape[1] // w_ref.shape[2]
    write_projections(h_ref, lambda j: w_ref[j], first, o_ref, row)


def teacher_project(blocks, mods, weights, first, olds=()):
    sizes = [b.shape[0] for b in blocks]
    rows, width = sum(sizes), blocks[0].shape[1]
    count, columns = 3 - first, weights.shape[2]
    total = rows + sum(o.shape[0] for o in olds)
    return pl.pallas_call(
        functools.partial(teacher_kernel, sizes, len(olds)),
        out_shape=[
            jax.ShapeDtypeStruct((total, count * columns), BF16),
            jax.ShapeDtypeStruct((rows, width), BF16),
        ],
        scratch_shapes=[pltpu.VMEM((rows, width), BF16)],
        compiler_params=pltpu.CompilerParams(vmem_limit_bytes=VMEM),
        cost_estimate=pl.CostEstimate(
            flops=rows * width * columns * count // 4,
            bytes_accessed=rows * width,
            transcendentals=0,
        ),
        name="teacher_project",
    )(*blocks, *mods, weights, *olds)


def critic_kernel(firsts, *refs):
    hs, (w_ref, o_ref) = refs[: len(firsts)], refs[len(firsts) :]
    row = 0
    for h_ref, first in zip(hs, firsts):
        width = h_ref.shape[1]
        write_projections(
            h_ref, lambda j, width=width: w_ref[:, j].reshape(width, -1), first, o_ref, row
        )
        row += h_ref.shape[0]


def critic_project(hs, weights, firsts):
    rows, width = sum(h.shape[0] for h in hs), hs[0].shape[1]
    columns = weights.shape[3]
    return pl.pallas_call(
        functools.partial(critic_kernel, firsts),
        out_shape=jax.ShapeDtypeStruct((rows, 3 * columns), BF16),
        compiler_params=pltpu.CompilerParams(vmem_limit_bytes=VMEM),
        cost_estimate=pl.CostEstimate(
            flops=rows * width * columns,
            bytes_accessed=rows * width,
            transcendentals=0,
        ),
        name="critic_project",
    )(*hs, weights)


def attend_kernel(places, groups, sums, *refs):
    models, (wt_ref, wc_ref), refs = (
        (refs[:groups], refs[groups : 2 * groups]),
        refs[2 * groups : 2 * groups + 2],
        refs[2 * groups + 2 :],
    )
    arrived, outs, o_ref = refs[: len(sums)], refs[len(sums) : -1], refs[-1]
    columns, width = wt_ref.shape
    for m, keyed in enumerate(models):
        for head in range(columns // HEAD_DIM):
            base = head * HEAD_DIM
            query = jnp.concatenate(
                [keyed[g][pl.ds(row, HALF), pl.ds(base, HEAD_DIM)] for g, row in places], axis=0
            )
            parts = [
                [
                    ref[:, pl.ds(ref.shape[1] - n * columns + base, HEAD_DIM)]
                    for n in (2, 1)
                ]
                for ref in keyed
            ]
            scores = [
                lax.dot_general(
                    query, k, (((1,), (1,)), ((), ())), preferred_element_type=F32
                )
                for k, _ in parts
            ]
            top = functools.reduce(
                jnp.maximum, [jnp.max(s, axis=1, keepdims=True) for s in scores]
            )
            mixed = 0.0
            for s, (_, v) in zip(scores, parts):
                prob = jnp.exp2(s - top).astype(BF16)
                with_ones = jnp.concatenate([v, jnp.ones_like(v)], axis=1)
                mixed = mixed + jnp.dot(prob, with_ones, preferred_element_type=F32)
            o_ref[:, pl.ds(m * columns + head * HEAD_DIM, HEAD_DIM)] = (
                mixed[:, :HEAD_DIM] / mixed[:, HEAD_DIM:]
            ).astype(BF16)
    critic = wc_ref[...].reshape(width, columns)
    part = width // 4
    for j in range(4):
        at = pl.ds(j * part, part)
        diff = lax.dot_general(
            o_ref[:, columns:],
            critic[j * part : (j + 1) * part],
            (((1,), (1,)), ((), ())),
            preferred_element_type=F32,
        ) - jnp.dot(o_ref[:, :columns], wt_ref[:, at], preferred_element_type=F32)
        for i, arrival in zip(sums, arrived):
            add = arrival[:, at].astype(F32)
            rows = [diff[: i * HALF], diff[i * HALF : (i + 1) * HALF] + add, diff[(i + 1) * HALF :]]
            diff = jnp.concatenate([r for r in rows if r.shape[0]], axis=0)
        base = 0
        for out in outs:
            out[:, at] = diff[base : base + out.shape[0]].astype(out.dtype)
            base += out.shape[0]


def attend(places, split, teacher, critic, teacher_out, critic_out, arrived=None):
    arrived = arrived or {}
    rows = HALF * len(places)
    columns, width = teacher_out.shape
    keys = sum(g.shape[0] for g in teacher)

    args = (*teacher, *critic, teacher_out, critic_out, *arrived.values())
    return pl.pallas_call(
        functools.partial(attend_kernel, places, len(teacher), tuple(arrived)),
        out_shape=[jax.ShapeDtypeStruct((n * HALF, width), BF16) for n in split],
        scratch_shapes=[pltpu.VMEM((rows, 2 * columns), BF16)],
        compiler_params=pltpu.CompilerParams(vmem_limit_bytes=VMEM),
        cost_estimate=pl.CostEstimate(
            flops=8 * rows * columns * (2 * keys + width),
            bytes_accessed=rows * width,
            transcendentals=0,
        ),
        name="attend",
    )(*args)


def shards(
    latents,
    noise,
    tsteps,
    text,
    teacher_qkv,
    teacher_out,
    teacher_mod,
    critic_qkv,
    critic_out,
    critic_mod,
):
    images = latents.shape[0]
    n_dp, n_head = lax.axis_size("dp"), lax.axis_size("head")
    dp, head = lax.axis_index("dp"), lax.axis_index("head")
    core = dp % 2

    local_times = lax.dynamic_slice_in_dim(tsteps, head * images, images)
    sigma = (local_times.astype(F32) / 1000.0)[:, None, None]
    noisy = ((1.0 - sigma) * latents.astype(F32) + sigma * noise.astype(F32)).astype(BF16)

    def cross(flip):
        return [
            (d * n_head + h, (2 * h + (d % 2) ^ flip) * n_head + d // 2)
            for d in range(n_dp)
            for h in range(n_head)
        ]

    first = jnp.where(core == 0, noisy[0], noisy[1])
    second = jnp.where(core == 0, noisy[1], noisy[0])
    up = [(i, (i + 2) % n_head) for i in range(n_head)]
    down = [(i, (i - 2) % n_head) for i in range(n_head)]
    twice = [(i, (i + 4) % n_head) for i in range(n_head)]
    swap = [(i, i ^ 1) for i in range(n_head)]

    def go(x, perm):
        return lax.ppermute(x, "head", perm)

    fence = lax.optimization_barrier
    own_time = lax.dynamic_slice_in_dim(tsteps, dp, 1)
    temb = embed(own_time, teacher_mod.shape[0])
    mods = [modulation(temb, w) for w in (teacher_mod, critic_mod)]
    w_critic = lax.all_gather(critic_qkv, "dp")


    own_0 = lax.ppermute(first, ("dp", "head"), cross(0))
    text_t, text_h = teacher_project([text[0]], mods, teacher_qkv, 1)
    own_0, text_t, text_h = fence((own_0, text_t, text_h))

    own_1 = lax.ppermute(second, ("dp", "head"), cross(1))
    below_0, above_0, other_0 = go(own_0, up), go(own_0, down), go(own_0, swap)
    own_0, own_1, below_0, above_0, other_0 = fence((own_0, own_1, below_0, above_0, other_0))

    below_1, above_1, other_1 = go(own_1, up), go(own_1, down), go(own_1, swap)
    far_0, far_1 = go(below_0, up), go(own_1, twice)
    t_1, h_1 = teacher_project([own_0, own_1, below_0, above_0, other_0], mods, teacher_qkv, 0)
    other = jnp.concatenate([other_0, other_1], axis=0)
    far = jnp.concatenate([far_0, far_1], axis=0)
    below_1, above_1, other, far, t_1, text_h = fence((below_1, above_1, other, far, t_1, text_h))
    w_critic, out_t, text_h = fence((w_critic, critic_out.T, text_h))

    w_critic_out = lax.all_gather(out_t, "dp")
    o_below, o_above, o_far = go(other, up), go(other, down), go(far, swap)
    blocks = [below_1, above_1, other[HALF:], far]
    t_early, h_2 = teacher_project(blocks, mods, teacher_qkv, 0, [text_t, t_1])
    c_early = critic_project([text_h, h_1, h_2], w_critic, (1, 0, 0))
    o_below, o_above, o_far, c_early = fence((o_below, o_above, o_far, c_early))
    t_3, h_3 = teacher_project([o_below, o_above, o_far], mods, teacher_qkv, 0)
    c_3 = critic_project([h_3], w_critic, (0,))
    teacher, critic = [t_early, t_3], [c_early, c_3]

    def run(places, split, arrived=None):
        places = [(int(g == 3), (0, 512, 832, 0)[g] + HALF * i) for g, i in places]
        return attend(places, split, teacher, critic, teacher_out, w_critic_out, arrived)

    def add(*parts):
        return functools.reduce(jnp.add, [p.astype(F32) for p in parts]).astype(BF16)

    fo_a, fo_b = run([(3, 4), (3, 5)], [1, 1])
    via_o_a, via_o_b = go(fo_a, up), go(fo_b, down)
    *teacher, fo_a = fence((*teacher, fo_a))
    f_a, f_b = run([(2, 3), (2, 4)], [1, 1])
    via_a, via_b = go(f_a, up), go(f_b, down)
    *teacher, f_a = fence((*teacher, f_a))
    ob, oa = run([(3, 0), (3, 1), (3, 2), (3, 3)], [2, 2], {1: via_o_b, 2: via_o_a})
    so_below, so_above = go(ob, down), go(oa, up)
    *teacher, ob = fence((*teacher, ob))
    nb, na = run([(1, 2), (2, 0), (1, 3), (2, 1)], [2, 2], {1: via_b, 2: via_a})
    s_below, s_above = go(nb, down), go(na, up)
    *teacher, _ = fence((*teacher, nb))
    ho, here = run([(1, 4), (2, 2), (1, 0), (1, 1)], [2, 2])
    crossed = go(add(ho, so_below, so_above), swap)
    out = add(here, s_below, s_above, crossed)
    out = jnp.where(core == 0, out, jnp.concatenate([out[HALF:], out[:HALF]], axis=0))
    return out[None]


def solution(mesh):
    in_specs = (
        P("head", "dp", None),
        P("head", "dp", None),
        P(),
        P("dp", None, None),
        P(None, None, "head"),
        P("head", None),
        P(),
        P(None, "dp", "head"),
        P("head", "dp"),
        P(),
    )
    out_specs = P("dp", "head", None)
    return jax.shard_map(shards, mesh=mesh, in_specs=in_specs, out_specs=out_specs, check_vma=False)
```

```python
import functools
import math

import jax
import jax.numpy as jnp
from jax import lax
from jax.experimental import pallas as pl
from jax.experimental.pallas import tpu as pltpu
from jax.sharding import PartitionSpec as P

HEAD_DIM = 128
HALF = 64
F32 = jnp.float32
BF16 = jnp.bfloat16
VMEM = 10 << 20
CHUNK = 64


def embed(tvals, width):
    half = width // 2
    freqs = jnp.exp(-math.log(10000.0) * jnp.arange(half, dtype=F32) / half)
    angle = tvals.astype(F32)[:, None] * freqs[None, :]
    return jnp.concatenate([jnp.cos(angle), jnp.sin(angle)], axis=1)


def modulation(temb, w_mod):
    act = jax.nn.silu(temb).astype(BF16)
    mod = jnp.dot(act, w_mod, preferred_element_type=F32)
    return mod.reshape(2, w_mod.shape[1] // 2)


def normalise(x_ref, mods, outs, base, size, chunk):
    def step(i, _):
        start = pl.multiple_of(i * chunk, chunk)
        rows = x_ref[pl.ds(start, chunk), :].astype(F32)
        pivot = rows[:, 0:1]
        away = rows - pivot
        mean = jnp.mean(away, axis=1, keepdims=True)
        var = jnp.maximum(jnp.mean(away * away, axis=1, keepdims=True) - mean * mean, 0.0)
        scale = lax.rsqrt(var + 1e-06)
        norm = (x_ref[pl.ds(start, chunk), :].astype(F32) - (pivot + mean)) * scale
        at = pl.ds(pl.multiple_of(base + start, chunk), chunk)
        for mod_ref, h_ref in zip(mods, outs):
            h_ref[at, :] = (norm * (1.0 + mod_ref[1:2, :]) + mod_ref[0:1, :]).astype(BF16)
        return 0

    lax.fori_loop(0, size // chunk, step, 0)


def write_projections(h_ref, weight_of, first, o_ref, row):
    columns = weight_of(0).shape[1]
    before = o_ref.shape[1] - 3 * columns

    def step(j, _):
        out = jnp.dot(h_ref[...], weight_of(j), preferred_element_type=F32)
        if first == 0:
            out = out * jnp.where(j == 0, math.log2(math.e) / math.sqrt(HEAD_DIM), 1.0)
        at = pl.ds(pl.multiple_of(j * columns + before, columns), columns)
        o_ref[row : row + h_ref.shape[0], at] = out.astype(BF16)
        return 0

    lax.fori_loop(first, 3, step, 0)


def teacher_kernel(sizes, kept, *refs):
    xs, refs = refs[: len(sizes)], refs[len(sizes) :]
    mods, w_ref, refs = refs[:2], refs[2], refs[3:]
    olds, (o_ref, hc_ref, h_ref) = refs[:kept], refs[kept:]
    base = 0
    for x_ref, size in zip(xs, sizes):
        normalise(x_ref, mods, (h_ref, hc_ref), base, size, CHUNK)
        base += size
    row = 0
    for old in olds:
        o_ref[row : row + old.shape[0], o_ref.shape[1] - old.shape[1] :] = old[...]
        row += old.shape[0]
    first = 3 - o_ref.shape[1] // w_ref.shape[2]
    write_projections(h_ref, lambda j: w_ref[j], first, o_ref, row)


def teacher_project(blocks, mods, weights, first, olds=()):
    sizes = [b.shape[0] for b in blocks]
    rows, width = sum(sizes), blocks[0].shape[1]
    count, columns = 3 - first, weights.shape[2]
    total = rows + sum(o.shape[0] for o in olds)
    return pl.pallas_call(
        functools.partial(teacher_kernel, sizes, len(olds)),
        out_shape=[
            jax.ShapeDtypeStruct((total, count * columns), BF16),
            jax.ShapeDtypeStruct((rows, width), BF16),
        ],
        scratch_shapes=[pltpu.VMEM((rows, width), BF16)],
        compiler_params=pltpu.CompilerParams(vmem_limit_bytes=VMEM),
        cost_estimate=pl.CostEstimate(
            flops=rows * width * columns * count // 4,
            bytes_accessed=rows * width,
            transcendentals=0,
        ),
        name="teacher_project",
    )(*blocks, *mods, weights, *olds)


def critic_kernel(firsts, *refs):
    hs, (w_ref, o_ref) = refs[: len(firsts)], refs[len(firsts) :]
    row = 0
    for h_ref, first in zip(hs, firsts):
        width = h_ref.shape[1]
        write_projections(
            h_ref, lambda j, width=width: w_ref[:, j].reshape(width, -1), first, o_ref, row
        )
        row += h_ref.shape[0]


def critic_project(hs, weights, firsts):
    rows, width = sum(h.shape[0] for h in hs), hs[0].shape[1]
    columns = weights.shape[3]
    return pl.pallas_call(
        functools.partial(critic_kernel, firsts),
        out_shape=jax.ShapeDtypeStruct((rows, 3 * columns), BF16),
        compiler_params=pltpu.CompilerParams(vmem_limit_bytes=VMEM),
        cost_estimate=pl.CostEstimate(
            flops=rows * width * columns,
            bytes_accessed=rows * width,
            transcendentals=0,
        ),
        name="critic_project",
    )(*hs, weights)


def attend_kernel(places, groups, sums, *refs):
    models, (wt_ref, wc_ref), refs = (
        (refs[:groups], refs[groups : 2 * groups]),
        refs[2 * groups : 2 * groups + 2],
        refs[2 * groups + 2 :],
    )
    arrived, outs, o_ref = refs[: len(sums)], refs[len(sums) : -1], refs[-1]
    columns, width = wt_ref.shape
    for m, keyed in enumerate(models):
        for head in range(columns // HEAD_DIM):
            base = head * HEAD_DIM
            query = jnp.concatenate(
                [keyed[g][pl.ds(row, HALF), pl.ds(base, HEAD_DIM)] for g, row in places], axis=0
            )
            parts = [
                [
                    ref[:, pl.ds(ref.shape[1] - n * columns + base, HEAD_DIM)]
                    for n in (2, 1)
                ]
                for ref in keyed
            ]
            scores = [
                lax.dot_general(
                    query, k, (((1,), (1,)), ((), ())), preferred_element_type=F32
                )
                for k, _ in parts
            ]
            top = functools.reduce(
                jnp.maximum, [jnp.max(s, axis=1, keepdims=True) for s in scores]
            )
            mixed = 0.0
            for s, (_, v) in zip(scores, parts):
                prob = jnp.exp2(s - top).astype(BF16)
                with_ones = jnp.concatenate([v, jnp.ones_like(v)], axis=1)
                mixed = mixed + jnp.dot(prob, with_ones, preferred_element_type=F32)
            o_ref[:, pl.ds(m * columns + head * HEAD_DIM, HEAD_DIM)] = (
                mixed[:, :HEAD_DIM] / mixed[:, HEAD_DIM:]
            ).astype(BF16)
    critic = wc_ref[...].reshape(width, columns)
    part = width // 4
    for j in range(4):
        at = pl.ds(j * part, part)
        diff = lax.dot_general(
            o_ref[:, columns:],
            critic[j * part : (j + 1) * part],
            (((1,), (1,)), ((), ())),
            preferred_element_type=F32,
        ) - jnp.dot(o_ref[:, :columns], wt_ref[:, at], preferred_element_type=F32)
        for i, arrival in zip(sums, arrived):
            add = arrival[:, at].astype(F32)
            rows = [diff[: i * HALF], diff[i * HALF : (i + 1) * HALF] + add, diff[(i + 1) * HALF :]]
            diff = jnp.concatenate([r for r in rows if r.shape[0]], axis=0)
        base = 0
        for out in outs:
            out[:, at] = diff[base : base + out.shape[0]].astype(out.dtype)
            base += out.shape[0]


def attend(places, split, teacher, critic, teacher_out, critic_out, arrived=None):
    arrived = arrived or {}
    rows = HALF * len(places)
    columns, width = teacher_out.shape
    keys = sum(g.shape[0] for g in teacher)

    args = (*teacher, *critic, teacher_out, critic_out, *arrived.values())
    return pl.pallas_call(
        functools.partial(attend_kernel, places, len(teacher), tuple(arrived)),
        out_shape=[jax.ShapeDtypeStruct((n * HALF, width), BF16) for n in split],
        scratch_shapes=[pltpu.VMEM((rows, 2 * columns), BF16)],
        compiler_params=pltpu.CompilerParams(vmem_limit_bytes=VMEM),
        cost_estimate=pl.CostEstimate(
            flops=8 * rows * columns * (2 * keys + width),
            bytes_accessed=rows * width,
            transcendentals=0,
        ),
        name="attend",
    )(*args)


def shards(
    latents,
    noise,
    tsteps,
    text,
    teacher_qkv,
    teacher_out,
    teacher_mod,
    critic_qkv,
    critic_out,
    critic_mod,
):
    images = latents.shape[0]
    n_dp, n_head = lax.axis_size("dp"), lax.axis_size("head")
    dp, head = lax.axis_index("dp"), lax.axis_index("head")
    core = dp % 2

    local_times = lax.dynamic_slice_in_dim(tsteps, head * images, images)
    sigma = (local_times.astype(F32) / 1000.0)[:, None, None]
    noisy = ((1.0 - sigma) * latents.astype(F32) + sigma * noise.astype(F32)).astype(BF16)

    def cross(flip):
        return [
            (d * n_head + h, (2 * h + (d % 2) ^ flip) * n_head + d // 2)
            for d in range(n_dp)
            for h in range(n_head)
        ]

    first = jnp.where(core == 0, noisy[0], noisy[1])
    second = jnp.where(core == 0, noisy[1], noisy[0])
    up = [(i, (i + 2) % n_head) for i in range(n_head)]
    down = [(i, (i - 2) % n_head) for i in range(n_head)]
    twice = [(i, (i + 4) % n_head) for i in range(n_head)]
    swap = [(i, i ^ 1) for i in range(n_head)]

    def go(x, perm):
        return lax.ppermute(x, "head", perm)

    fence = lax.optimization_barrier
    own_time = lax.dynamic_slice_in_dim(tsteps, dp, 1)
    temb = embed(own_time, teacher_mod.shape[0])
    mods = [modulation(temb, w) for w in (teacher_mod, critic_mod)]
    w_critic = lax.all_gather(critic_qkv, "dp")


    own_0 = lax.ppermute(first, ("dp", "head"), cross(0))
    text_t, text_h = teacher_project([text[0]], mods, teacher_qkv, 1)
    own_0, text_t, text_h = fence((own_0, text_t, text_h))

    own_1 = lax.ppermute(second, ("dp", "head"), cross(1))
    below_0, above_0, other_0 = go(own_0, up), go(own_0, down), go(own_0, swap)
    own_0, own_1, below_0, above_0, other_0 = fence((own_0, own_1, below_0, above_0, other_0))

    below_1, above_1, other_1 = go(own_1, up), go(own_1, down), go(own_1, swap)
    far_0, far_1 = go(below_0, up), go(own_1, twice)
    t_1, h_1 = teacher_project([own_0, own_1, below_0, above_0, other_0], mods, teacher_qkv, 0)
    other = jnp.concatenate([other_0, other_1], axis=0)
    far = jnp.concatenate([far_0, far_1], axis=0)
    below_1, above_1, other_1, t_1 = fence((below_1, above_1, other_1, t_1))
    t_2, h_2 = teacher_project([below_1, above_1, other_1], mods, teacher_qkv, 0)
    other, far, t_1, t_2, text_h = fence((other, far, t_1, t_2, text_h))
    w_critic, out_t, text_h = fence((w_critic, critic_out.T, text_h))

    w_critic_out = lax.all_gather(out_t, "dp")
    o_below, o_above, o_far = go(other, up), go(other, down), go(far, swap)
    t_early, h_3 = teacher_project([far], mods, teacher_qkv, 0, [text_t, t_1, t_2])
    c_early = critic_project([text_h, h_1, h_2, h_3], w_critic, (1, 0, 0, 0))
    o_below, o_above, o_far, c_early = fence((o_below, o_above, o_far, c_early))
    t_late, h_4 = teacher_project([o_below, o_above, o_far], mods, teacher_qkv, 0)
    c_late = critic_project([h_4], w_critic, (0,))
    teacher, critic = [t_early, t_late], [c_early, c_late]

    def run(places, split, arrived=None):
        places = [(int(g == 3), (0, 512, 832, 0)[g] + HALF * i) for g, i in places]
        return attend(places, split, teacher, critic, teacher_out, w_critic_out, arrived)

    def add(*parts):
        return functools.reduce(jnp.add, [p.astype(F32) for p in parts]).astype(BF16)

    fo_a, fo_b = run([(3, 4), (3, 5)], [1, 1])
    via_o_a, via_o_b = go(fo_a, up), go(fo_b, down)
    *teacher, fo_a = fence((*teacher, fo_a))
    f_a, f_b = run([(2, 3), (2, 4)], [1, 1])
    via_a, via_b = go(f_a, up), go(f_b, down)
    *teacher, f_a = fence((*teacher, f_a))
    ob, oa = run([(3, 0), (3, 1), (3, 2), (3, 3)], [2, 2], {1: via_o_b, 2: via_o_a})
    so_below, so_above = go(ob, down), go(oa, up)
    *teacher, ob = fence((*teacher, ob))
    nb, na = run([(1, 2), (2, 0), (1, 3), (2, 1)], [2, 2], {1: via_b, 2: via_a})
    s_below, s_above = go(nb, down), go(na, up)
    *teacher, _ = fence((*teacher, nb))
    ho, here = run([(1, 4), (2, 2), (1, 0), (1, 1)], [2, 2])
    crossed = go(add(ho, so_below, so_above), swap)
    out = add(here, s_below, s_above, crossed)
    out = jnp.where(core == 0, out, jnp.concatenate([out[HALF:], out[:HALF]], axis=0))
    return out[None]


def solution(mesh):
    in_specs = (
        P("head", "dp", None),
        P("head", "dp", None),
        P(),
        P("dp", None, None),
        P(None, None, "head"),
        P("head", None),
        P(),
        P(None, "dp", "head"),
        P("head", "dp"),
        P(),
    )
    out_specs = P("dp", "head", None)
    return jax.shard_map(shards, mesh=mesh, in_specs=in_specs, out_specs=out_specs, check_vma=False)
```

```python
import functools
import math

import jax
import jax.numpy as jnp
from jax import lax
from jax.experimental import pallas as pl
from jax.experimental.pallas import tpu as pltpu
from jax.sharding import PartitionSpec as P

HEAD_DIM = 128
HALF = 64
F32 = jnp.float32
BF16 = jnp.bfloat16
VMEM = 10 << 20
CHUNK = 64


def embed(tvals, width):
    half = width // 2
    freqs = jnp.exp(-math.log(10000.0) * jnp.arange(half, dtype=F32) / half)
    angle = tvals.astype(F32)[:, None] * freqs[None, :]
    return jnp.concatenate([jnp.cos(angle), jnp.sin(angle)], axis=1)


def modulation(temb, w_mod):
    act = jax.nn.silu(temb).astype(BF16)
    mod = jnp.dot(act, w_mod, preferred_element_type=F32)
    return mod.reshape(2, w_mod.shape[1] // 2)


def normalise(x_ref, mods, outs, base, size, chunk):
    def step(i, _):
        start = pl.multiple_of(i * chunk, chunk)
        rows = x_ref[pl.ds(start, chunk), :].astype(F32)
        pivot = rows[:, 0:1]
        away = rows - pivot
        mean = jnp.mean(away, axis=1, keepdims=True)
        var = jnp.maximum(jnp.mean(away * away, axis=1, keepdims=True) - mean * mean, 0.0)
        scale = lax.rsqrt(var + 1e-06)
        norm = (x_ref[pl.ds(start, chunk), :].astype(F32) - (pivot + mean)) * scale
        at = pl.ds(pl.multiple_of(base + start, chunk), chunk)
        for mod_ref, h_ref in zip(mods, outs):
            h_ref[at, :] = (norm * (1.0 + mod_ref[1:2, :]) + mod_ref[0:1, :]).astype(BF16)
        return 0

    lax.fori_loop(0, size // chunk, step, 0)


def write_projections(h_ref, weight_of, first, o_ref, row):
    columns = weight_of(0).shape[1]
    before = o_ref.shape[1] - 3 * columns
    rows = slice(row, row + h_ref.shape[0])
    if first == 0:
        out = jnp.dot(h_ref[...], weight_of(0), preferred_element_type=F32)
        out = out * (math.log2(math.e) / math.sqrt(HEAD_DIM))
        o_ref[rows, before : before + columns] = out.astype(BF16)
    both = jnp.concatenate([weight_of(1), weight_of(2)], axis=1)
    out = jnp.dot(h_ref[...], both, preferred_element_type=F32)
    o_ref[rows, before + columns :] = out.astype(BF16)


def teacher_kernel(sizes, kept, *refs):
    xs, refs = refs[: len(sizes)], refs[len(sizes) :]
    mods, w_ref, refs = refs[:2], refs[2], refs[3:]
    olds, (o_ref, hc_ref, h_ref) = refs[:kept], refs[kept:]
    base = 0
    for x_ref, size in zip(xs, sizes):
        normalise(x_ref, mods, (h_ref, hc_ref), base, size, CHUNK)
        base += size
    row = 0
    for old in olds:
        o_ref[row : row + old.shape[0], o_ref.shape[1] - old.shape[1] :] = old[...]
        row += old.shape[0]
    first = 3 - o_ref.shape[1] // w_ref.shape[2]
    write_projections(h_ref, lambda j: w_ref[j], first, o_ref, row)


def teacher_project(blocks, mods, weights, first, olds=()):
    sizes = [b.shape[0] for b in blocks]
    rows, width = sum(sizes), blocks[0].shape[1]
    count, columns = 3 - first, weights.shape[2]
    total = rows + sum(o.shape[0] for o in olds)
    return pl.pallas_call(
        functools.partial(teacher_kernel, sizes, len(olds)),
        out_shape=[
            jax.ShapeDtypeStruct((total, count * columns), BF16),
            jax.ShapeDtypeStruct((rows, width), BF16),
        ],
        scratch_shapes=[pltpu.VMEM((rows, width), BF16)],
        compiler_params=pltpu.CompilerParams(vmem_limit_bytes=VMEM),
        cost_estimate=pl.CostEstimate(
            flops=rows * width * columns * count // 4,
            bytes_accessed=rows * width,
            transcendentals=0,
        ),
        name="teacher_project",
    )(*blocks, *mods, weights, *olds)


def critic_kernel(firsts, *refs):
    hs, (w_ref, o_ref) = refs[: len(firsts)], refs[len(firsts) :]
    row = 0
    for h_ref, first in zip(hs, firsts):
        width = h_ref.shape[1]
        write_projections(
            h_ref, lambda j, width=width: w_ref[:, j].reshape(width, -1), first, o_ref, row
        )
        row += h_ref.shape[0]


def critic_project(hs, weights, firsts):
    rows, width = sum(h.shape[0] for h in hs), hs[0].shape[1]
    columns = weights.shape[3]
    return pl.pallas_call(
        functools.partial(critic_kernel, firsts),
        out_shape=jax.ShapeDtypeStruct((rows, 3 * columns), BF16),
        compiler_params=pltpu.CompilerParams(vmem_limit_bytes=VMEM),
        cost_estimate=pl.CostEstimate(
            flops=rows * width * columns,
            bytes_accessed=rows * width,
            transcendentals=0,
        ),
        name="critic_project",
    )(*hs, weights)


def attend_kernel(places, groups, sums, *refs):
    models, (wt_ref, wc_ref), refs = (
        (refs[:groups], refs[groups : 2 * groups]),
        refs[2 * groups : 2 * groups + 2],
        refs[2 * groups + 2 :],
    )
    arrived, outs, o_ref = refs[: len(sums)], refs[len(sums) : -1], refs[-1]
    columns, width = wt_ref.shape
    for m, keyed in enumerate(models):
        for head in range(columns // HEAD_DIM):
            base = head * HEAD_DIM
            query = jnp.concatenate(
                [keyed[g][pl.ds(row, HALF), pl.ds(base, HEAD_DIM)] for g, row in places], axis=0
            )
            parts = [
                [
                    ref[:, pl.ds(ref.shape[1] - n * columns + base, HEAD_DIM)]
                    for n in (2, 1)
                ]
                for ref in keyed
            ]
            scores = [
                lax.dot_general(
                    query, k, (((1,), (1,)), ((), ())), preferred_element_type=F32
                )
                for k, _ in parts
            ]
            top = functools.reduce(
                jnp.maximum, [jnp.max(s, axis=1, keepdims=True) for s in scores]
            )
            mixed = 0.0
            for s, (_, v) in zip(scores, parts):
                prob = jnp.exp2(s - top).astype(BF16)
                with_ones = jnp.concatenate([v, jnp.ones_like(v)], axis=1)
                mixed = mixed + jnp.dot(prob, with_ones, preferred_element_type=F32)
            o_ref[:, pl.ds(m * columns + head * HEAD_DIM, HEAD_DIM)] = (
                mixed[:, :HEAD_DIM] / mixed[:, HEAD_DIM:]
            ).astype(BF16)
    critic = wc_ref[...].reshape(width, columns)
    part = width // 4
    for j in range(4):
        at = pl.ds(j * part, part)
        diff = lax.dot_general(
            o_ref[:, columns:],
            critic[j * part : (j + 1) * part],
            (((1,), (1,)), ((), ())),
            preferred_element_type=F32,
        ) - jnp.dot(o_ref[:, :columns], wt_ref[:, at], preferred_element_type=F32)
        for i, arrival in zip(sums, arrived):
            add = arrival[:, at].astype(F32)
            rows = [diff[: i * HALF], diff[i * HALF : (i + 1) * HALF] + add, diff[(i + 1) * HALF :]]
            diff = jnp.concatenate([r for r in rows if r.shape[0]], axis=0)
        base = 0
        for out in outs:
            out[:, at] = diff[base : base + out.shape[0]].astype(out.dtype)
            base += out.shape[0]


def attend(places, split, teacher, critic, teacher_out, critic_out, arrived=None):
    arrived = arrived or {}
    rows = HALF * len(places)
    columns, width = teacher_out.shape
    keys = sum(g.shape[0] for g in teacher)

    args = (*teacher, *critic, teacher_out, critic_out, *arrived.values())
    return pl.pallas_call(
        functools.partial(attend_kernel, places, len(teacher), tuple(arrived)),
        out_shape=[jax.ShapeDtypeStruct((n * HALF, width), BF16) for n in split],
        scratch_shapes=[pltpu.VMEM((rows, 2 * columns), BF16)],
        compiler_params=pltpu.CompilerParams(vmem_limit_bytes=VMEM),
        cost_estimate=pl.CostEstimate(
            flops=8 * rows * columns * (2 * keys + width),
            bytes_accessed=rows * width,
            transcendentals=0,
        ),
        name="attend",
    )(*args)


def shards(
    latents,
    noise,
    tsteps,
    text,
    teacher_qkv,
    teacher_out,
    teacher_mod,
    critic_qkv,
    critic_out,
    critic_mod,
):
    images = latents.shape[0]
    n_dp, n_head = lax.axis_size("dp"), lax.axis_size("head")
    dp, head = lax.axis_index("dp"), lax.axis_index("head")
    core = dp % 2

    local_times = lax.dynamic_slice_in_dim(tsteps, head * images, images)
    sigma = (local_times.astype(F32) / 1000.0)[:, None, None]
    noisy = ((1.0 - sigma) * latents.astype(F32) + sigma * noise.astype(F32)).astype(BF16)

    def cross(flip):
        return [
            (d * n_head + h, (2 * h + (d % 2) ^ flip) * n_head + d // 2)
            for d in range(n_dp)
            for h in range(n_head)
        ]

    first = jnp.where(core == 0, noisy[0], noisy[1])
    second = jnp.where(core == 0, noisy[1], noisy[0])
    up = [(i, (i + 2) % n_head) for i in range(n_head)]
    down = [(i, (i - 2) % n_head) for i in range(n_head)]
    twice = [(i, (i + 4) % n_head) for i in range(n_head)]
    swap = [(i, i ^ 1) for i in range(n_head)]

    def go(x, perm):
        return lax.ppermute(x, "head", perm)

    fence = lax.optimization_barrier
    own_time = lax.dynamic_slice_in_dim(tsteps, dp, 1)
    temb = embed(own_time, teacher_mod.shape[0])
    mods = [modulation(temb, w) for w in (teacher_mod, critic_mod)]
    w_critic = lax.all_gather(critic_qkv, "dp")


    own_0 = lax.ppermute(first, ("dp", "head"), cross(0))
    text_t, text_h = teacher_project([text[0]], mods, teacher_qkv, 1)
    own_0, text_t, text_h = fence((own_0, text_t, text_h))

    own_1 = lax.ppermute(second, ("dp", "head"), cross(1))
    below_0, above_0, other_0 = go(own_0, up), go(own_0, down), go(own_0, swap)
    own_0, own_1, below_0, above_0, other_0 = fence((own_0, own_1, below_0, above_0, other_0))

    below_1, above_1, other_1 = go(own_1, up), go(own_1, down), go(own_1, swap)
    far_0, far_1 = go(below_0, up), go(own_1, twice)
    t_1, h_1 = teacher_project([own_0, own_1, below_0, above_0, other_0], mods, teacher_qkv, 0)
    other = jnp.concatenate([other_0, other_1], axis=0)
    far = jnp.concatenate([far_0, far_1], axis=0)
    below_1, above_1, other_1, t_1 = fence((below_1, above_1, other_1, t_1))
    t_2, h_2 = teacher_project([below_1, above_1, other_1], mods, teacher_qkv, 0)
    other, far, t_1, t_2, text_h = fence((other, far, t_1, t_2, text_h))
    w_critic, out_t, text_h = fence((w_critic, critic_out.T, text_h))

    w_critic_out = lax.all_gather(out_t, "dp")
    o_below, o_above, o_far = go(other, up), go(other, down), go(far, swap)
    t_early, h_3 = teacher_project([far], mods, teacher_qkv, 0, [text_t, t_1, t_2])
    c_early = critic_project([text_h, h_1, h_2, h_3], w_critic, (1, 0, 0, 0))
    o_below, o_above, o_far, c_early = fence((o_below, o_above, o_far, c_early))
    t_late, h_4 = teacher_project([o_below, o_above, o_far], mods, teacher_qkv, 0)
    c_late = critic_project([h_4], w_critic, (0,))
    teacher, critic = [t_early, t_late], [c_early, c_late]

    def run(places, split, arrived=None):
        places = [(int(g == 3), (0, 512, 832, 0)[g] + HALF * i) for g, i in places]
        return attend(places, split, teacher, critic, teacher_out, w_critic_out, arrived)

    def add(*parts):
        return functools.reduce(jnp.add, [p.astype(F32) for p in parts]).astype(BF16)

    fo_a, fo_b = run([(3, 4), (3, 5)], [1, 1])
    via_o_a, via_o_b = go(fo_a, up), go(fo_b, down)
    *teacher, fo_a = fence((*teacher, fo_a))
    f_a, f_b = run([(2, 3), (2, 4)], [1, 1])
    via_a, via_b = go(f_a, up), go(f_b, down)
    *teacher, f_a = fence((*teacher, f_a))
    ob, oa = run([(3, 0), (3, 1), (3, 2), (3, 3)], [2, 2], {1: via_o_b, 2: via_o_a})
    so_below, so_above = go(ob, down), go(oa, up)
    *teacher, ob = fence((*teacher, ob))
    nb, na = run([(1, 2), (2, 0), (1, 3), (2, 1)], [2, 2], {1: via_b, 2: via_a})
    s_below, s_above = go(nb, down), go(na, up)
    *teacher, _ = fence((*teacher, nb))
    ho, here = run([(1, 4), (2, 2), (1, 0), (1, 1)], [2, 2])
    crossed = go(add(ho, so_below, so_above), swap)
    out = add(here, s_below, s_above, crossed)
    out = jnp.where(core == 0, out, jnp.concatenate([out[HALF:], out[:HALF]], axis=0))
    return out[None]


def solution(mesh):
    in_specs = (
        P("head", "dp", None),
        P("head", "dp", None),
        P(),
        P("dp", None, None),
        P(None, None, "head"),
        P("head", None),
        P(),
        P(None, "dp", "head"),
        P("head", "dp"),
        P(),
    )
    out_specs = P("dp", "head", None)
    return jax.shard_map(shards, mesh=mesh, in_specs=in_specs, out_specs=out_specs, check_vma=False)
```
